32 devices in a mesh: delay: 2 (over y), row: 4 (over x, core), col: 4 (over z).
Axes of the slice: x: 2, y: 2, z: 4, core: 2. Of those that a mesh axis runs over, the one named last changes fastest.
Arguments:
- excitation: bfloat16 [2, 3072, 128], P(None, 'row'), may hold values from -6 to 6
- delay_ops: bfloat16 [2, 3072, 3072], P('delay', 'row', 'col'), may hold values from -0.078125 to 0.078125
- inverse_op: bfloat16 [3072, 3072], P('col', 'row'), may hold values from -0.109375 to 0.109375
- history: bfloat16 [2, 3072, 128], P('delay', 'col'), may hold values from -6 to 6
Outputs:
- currents: bfloat16 [2, 3072, 128], P(None, 'col')
- final_history: bfloat16 [2, 3072, 128], P('delay', 'col')
The draws below stay inside these ranges and needn't reach their ends.
All inputs are finite; a program needn't handle non-finite values.
Results may differ from the reference program's by a relative error of at most 0.008.
Values may be sent and summed in bfloat16 or wider, within the bound.
No kernel may reach another device: no remote copies, remote signals or barrier semaphores. Data moves between devices by JAX's collectives and lax.ppermute only.
A program may use at most 64 MiB of HBM per device.

```python
import jax
import jax.numpy as jnp
from jax import lax

N = 3072
EXC = 128
STEPS = 2
DELAYS = 2


def steps_of(rng, dims, split, smallest, top_value):
    factor_of = 1.0
    for dim, shards_of in split:
        steps = jax.random.uniform(jax.random.fold_in(jax.random.fold_in(rng, 6), dim), (shards_of,), jnp.float32, smallest / len(split), top_value / len(split))
        factor_of = factor_of * jnp.repeat(jnp.exp(steps), dims[dim] // shards_of).reshape((-1,) + (1,) * (len(dims) - 1 - dim))
    return factor_of


def gaussian(own_key, dims, width, most, shards=(), kind=jnp.bfloat16):
    factor_of = steps_of(own_key, dims, shards, -0.22, 0.18) if shards else 1.0
    entries = jax.random.normal(own_key, dims, jnp.float32) * width * factor_of
    return jnp.minimum(jnp.maximum(entries, -most), most).astype(kind)


def setup_inputs(seed: int = 0) -> dict:
    keys = jax.random.split(jax.random.key(seed), 5)
    excitation = gaussian(keys[0], (STEPS, N, EXC), 1.0, 6.0, ((1, 4),))
    delay_ops = gaussian(keys[1], (DELAYS, N, N), (N * DELAYS) ** -0.5, 0.078125, ((0, 2), (1, 4), (2, 4)))
    inverse_op = gaussian(keys[2], (N, N), N ** -0.5, 0.109375, ((0, 4), (1, 4)))
    history = gaussian(keys[3], (DELAYS, N, EXC), 1.0, 6.0, ((0, 2), (1, 4)))
    return dict(excitation=excitation, delay_ops=delay_ops, inverse_op=inverse_op, history=history)


def reference(excitation, delay_ops, inverse_op, history):
    def advance(hist, incident):
        def add_delay(total, pair):
            operator, past = pair
            return total + jnp.dot(operator, past, preferred_element_type=jnp.float32), None

        start = jnp.zeros(hist.shape[1:], jnp.float32)
        retarded, unused = lax.scan(add_delay, start, (delay_ops, hist))
        rhs = (incident.astype(jnp.float32) - retarded).astype(jnp.bfloat16)
        current = jnp.dot(inverse_op, rhs, preferred_element_type=jnp.float32).astype(jnp.bfloat16)
        hist = jnp.concatenate([current[None], hist[:-1]], axis=0)
        return hist, current

    final_history, currents = lax.scan(advance, history, excitation)
    return currents, final_history
```

```python
import jax
import jax.numpy as jnp
from jax import lax
from jax.sharding import PartitionSpec as P

F32 = jnp.float32
BF16 = jnp.bfloat16


def routes(axis):
    n = lax.axis_size(axis)
    if n & (n - 1) == 0:
        return [[(i, i ^ k) for i in range(n)] for k in range(1, n)]
    return [[(i, (i + k) % n) for i in range(n)] for k in range(1, n)]


def tree_sum(blocks):
    while len(blocks) > 1:
        pairs = [a + b for a, b in zip(blocks[::2], blocks[1::2])]
        blocks = pairs + ([blocks[-1]] if len(blocks) % 2 else [])
    return blocks[0]


def exchange_sum(block, axis):
    block = lax.optimization_barrier(block)
    blocks = [block] + [lax.ppermute(block, axis, route) for route in routes(axis)]
    return tree_sum([b.astype(F32) for b in blocks])


def piece(block, index, rows):
    return lax.dynamic_slice_in_dim(block, index * rows, rows, 0)


def scatter_sum(block, axis):
    n = lax.axis_size(axis)
    rows = block.shape[0] // n
    me = lax.axis_index(axis)
    parts = [piece(block, me, rows)]
    for route in routes(axis):
        target = jnp.array([t for _, t in route])[me]
        parts.append(lax.ppermute(piece(block, target, rows), axis, route))
    return tree_sum([p.astype(F32) for p in parts])


def gather(block, axis):
    n = lax.axis_size(axis)
    rows = block.shape[0]
    me = lax.axis_index(axis)
    whole = jnp.zeros((n * rows,) + block.shape[1:], block.dtype)
    whole = lax.dynamic_update_slice_in_dim(whole, block, me * rows, 0)
    for route in routes(axis):
        source = jnp.array([s for s, _ in sorted(route, key=lambda pair: pair[1])])[me]
        whole = lax.dynamic_update_slice_in_dim(whole, lax.ppermute(block, axis, route), source * rows, 0)
    return whole


def from_behind(block, axis, distance):
    n = lax.axis_size(axis)
    route = [(i - distance, i) for i in range(n) if i >= distance]
    return lax.ppermute(block, axis, route) if route else jnp.zeros_like(block)


def spread(block, axis, source):
    me = lax.axis_index(axis)
    out = block
    for target in range(lax.axis_size(axis)):
        if target != source:
            out = jnp.where(me == target, lax.ppermute(block, axis, [(source, target)]), out)
    return out


def times_transposed(a, b):
    return lax.dot_general(a, b, (((1,), (1,)), ((), ())), preferred_element_type=F32)


def on_device(excitation, delay_ops, inverse_op, history):
    steps, _, exc = excitation.shape
    operator, stored = delay_ops[0], history[0]
    nd = lax.axis_size("delay")
    me = lax.axis_index("delay")
    share = exc // nd
    stored_t = stored.T
    older = [scatter_sum(times_transposed(stored_t, operator).astype(BF16), "delay")]
    for step in range(1, steps):
        earlier = from_behind(stored_t, "delay", step)
        older.append(scatter_sum(times_transposed(earlier, operator).astype(BF16), "delay"))
    shortest = [spread(operator, "delay", lag) for lag in range(min(steps - 1, nd))]
    incident = [piece(excitation[step].T, me, share).astype(F32) for step in range(steps)]
    produced = []
    for step in range(steps):
        total = older[step]
        for lag in range(min(step, nd)):
            total = total + times_transposed(produced[step - 1 - lag], shortest[lag])
        retarded = exchange_sum(total.astype(BF16), "col")
        rhs = (incident[step] - retarded).astype(BF16)
        current = exchange_sum(times_transposed(rhs, inverse_op).astype(BF16), "row").astype(BF16)
        produced.append(current)
    whole = [gather(current, "delay").T for current in produced]
    currents = jnp.stack(whole)
    newest_first = jnp.stack(whole[::-1])
    picked = lax.dynamic_index_in_dim(newest_first, jnp.clip(me, 0, steps - 1), 0, keepdims=False)
    if nd > steps:
        picked = jnp.where(me < steps, picked, from_behind(stored, "delay", steps))
    return currents, picked[None]


def solution(mesh):
    in_specs = (
        P(None, "row", None),
        P("delay", "row", "col"),
        P("col", "row"),
        P("delay", "col", None),
    )
    out_specs = (P(None, "col", None), P("delay", "col", None))
    return jax.shard_map(
        on_device, mesh=mesh, in_specs=in_specs, out_specs=out_specs, check_vma=False
    )
```

```python
import functools

import jax
import jax.numpy as jnp
from jax import lax
from jax.experimental import pallas as pl
from jax.experimental.pallas import tpu as pltpu
from jax.sharding import PartitionSpec as P

F32 = jnp.float32
BF16 = jnp.bfloat16
TILE_ROWS = 16


def routes(axis):
    n = lax.axis_size(axis)
    if n & (n - 1) == 0:
        return [[(i, i ^ k) for i in range(n)] for k in range(1, n)]
    return [[(i, (i + k) % n) for i in range(n)] for k in range(1, n)]


def tree_sum(blocks):
    while len(blocks) > 1:
        pairs = [a + b for a, b in zip(blocks[::2], blocks[1::2])]
        blocks = pairs + ([blocks[-1]] if len(blocks) % 2 else [])
    return blocks[0]


def exchange_sum(block, axis):
    block = lax.optimization_barrier(block)
    blocks = [block] + [lax.ppermute(block, axis, route) for route in routes(axis)]
    return tree_sum([b.astype(F32) for b in blocks])


def piece(block, index, rows):
    return lax.dynamic_slice_in_dim(block, index * rows, rows, 0)


def scatter_sum(block, axis):
    n = lax.axis_size(axis)
    rows = block.shape[0] // n
    me = lax.axis_index(axis)
    parts = [piece(block, me, rows)]
    for route in routes(axis):
        target = jnp.array([t for _, t in route])[me]
        parts.append(lax.ppermute(piece(block, target, rows), axis, route))
    return tree_sum([p.astype(F32) for p in parts])


def gather(block, axis):
    n = lax.axis_size(axis)
    rows = block.shape[0]
    me = lax.axis_index(axis)
    whole = jnp.zeros((n * rows,) + block.shape[1:], block.dtype)
    whole = lax.dynamic_update_slice_in_dim(whole, block, me * rows, 0)
    for route in routes(axis):
        source = jnp.array([s for s, _ in sorted(route, key=lambda pair: pair[1])])[me]
        whole = lax.dynamic_update_slice_in_dim(whole, lax.ppermute(block, axis, route), source * rows, 0)
    return whole


def from_behind(block, axis, distance):
    n = lax.axis_size(axis)
    route = [(i - distance, i) for i in range(n) if i >= distance]
    return lax.ppermute(block, axis, route) if route else jnp.zeros_like(block)


def spread(block, axis, source):
    me = lax.axis_index(axis)
    out = block
    for target in range(lax.axis_size(axis)):
        if target != source:
            out = jnp.where(me == target, lax.ppermute(block, axis, [(source, target)]), out)
    return out


def times_transposed(a, b):
    return lax.dot_general(a, b, (((1,), (1,)), ((), ())), preferred_element_type=F32)


def general(excitation, delay_ops, inverse_op, history):
    steps, _, exc = excitation.shape
    operator, stored = delay_ops[0], history[0]
    nd = lax.axis_size("delay")
    me = lax.axis_index("delay")
    share = exc // nd
    stored_t = stored.T
    older = [scatter_sum(times_transposed(stored_t, operator).astype(BF16), "delay")]
    for step in range(1, steps):
        earlier = from_behind(stored_t, "delay", step)
        older.append(scatter_sum(times_transposed(earlier, operator).astype(BF16), "delay"))
    shortest = [spread(operator, "delay", lag) for lag in range(min(steps - 1, nd))]
    incident = [piece(excitation[step].T, me, share).astype(F32) for step in range(steps)]
    produced = []
    for step in range(steps):
        total = older[step]
        for lag in range(min(step, nd)):
            total = total + times_transposed(produced[step - 1 - lag], shortest[lag])
        retarded = exchange_sum(total.astype(BF16), "col")
        rhs = (incident[step] - retarded).astype(BF16)
        current = exchange_sum(times_transposed(rhs, inverse_op).astype(BF16), "row").astype(BF16)
        produced.append(current)
    whole = [gather(current, "delay").T for current in produced]
    currents = jnp.stack(whole)
    newest_first = jnp.stack(whole[::-1])
    picked = lax.dynamic_index_in_dim(newest_first, jnp.clip(me, 0, steps - 1), 0, keepdims=False)
    if nd > steps:
        picked = jnp.where(me < steps, picked, from_behind(stored, "delay", steps))
    return currents, picked[None]


class Layout:
    def __init__(self):
        self.nd = lax.axis_size("delay")
        self.nr = lax.axis_size("row")
        self.nc = lax.axis_size("col")
        self.near = 2 if self.nr % 2 == 0 else 1
        self.far = self.nr // self.near
        self.d = lax.axis_index("delay")
        self.n = lax.axis_index("row") % self.near
        self.z = lax.axis_index("col")

    def move(self, block, kd=0, kf=0, kn=0, kz=0, only=None):
        pairs = []
        for d in range(self.nd) if only is None else only:
            for r in range(self.nr):
                for z in range(self.nc):
                    to = ((d ^ kd) * self.nr + (r ^ (kf * self.near + kn))) * self.nc + (z ^ kz)
                    pairs.append(((d * self.nr + r) * self.nc + z, to))
        return lax.ppermute(block, ("delay", "row", "col"), pairs)

    def owners(self):
        return [(self.n ^ kn) * self.nd + (self.d ^ kd) for kn in range(self.near) for kd in range(self.nd)]


def kernel_call(body, out_shape, info, inputs, loose=(), scratch=()):
    vmem = pl.BlockSpec(memory_space=pltpu.VMEM)
    return pl.pallas_call(
        functools.partial(body, len(loose)),
        out_shape=out_shape,
        in_specs=[pl.BlockSpec(memory_space=pltpu.SMEM)] + [pl.BlockSpec(memory_space=pl.ANY)] * len(loose) + [vmem] * len(inputs),
        out_specs=jax.tree.map(lambda _: vmem, out_shape),
        scratch_shapes=list(scratch),
        compiler_params=pltpu.CompilerParams(vmem_limit_bytes=24 << 20),
    )(jnp.stack(info), *loose, *inputs)


def total_of(refs):
    return tree_sum([ref[...].astype(F32) for ref in refs])


def part_of(ref, index, rows):
    return ref[pl.ds(pl.multiple_of(index * rows, rows), rows), :]


def begin_body(near, nd, loose, info, *refs):
    past_ref, operator_ref, incident_ref = refs[:3]
    count = near * nd
    pieces, (part_ref, *waves), (total, turned, first, later) = refs[3 : 3 + count], refs[3 + count : -4], refs[-4:]
    turned[...] = past_ref[...].astype(F32).T
    total[...] = times_transposed(turned[...].astype(BF16), operator_ref[...])
    first[...] = incident_ref[0].astype(F32).T * info[0].astype(F32)
    rows = pieces[0].shape[0]
    for kn in range(near):
        for kd in range(nd):
            k = kn * nd + kd
            value = part_of(total, info[2 + k], rows)
            if kd == 0:
                value = value - part_of(first, info[2 + k], rows)
            pieces[k][...] = value.astype(BF16)
    later[...] = incident_ref[1].astype(F32).T
    for kn in range(near):
        waves[kn][...] = part_of(later, info[2 + kn * nd], rows).astype(BF16)
    part_ref[...] = part_of(turned, info[1], part_ref.shape[0]).astype(BF16)


def begin(lay, past, operator, incident):
    columns, exc = past.shape
    rows = operator.shape[0]
    owners = lay.owners()
    share = exc // len(owners)
    info = [(lay.z == 0).astype(jnp.int32), lay.n, *owners]
    out = [jax.ShapeDtypeStruct((share, rows), BF16)] * len(owners)
    out += [jax.ShapeDtypeStruct((share * lay.nd, columns), BF16)]
    out += [jax.ShapeDtypeStruct((share, rows), BF16)] * lay.near
    scratch = [pltpu.VMEM((exc, rows), F32), pltpu.VMEM((exc, columns), F32)] + [pltpu.VMEM((exc, rows), F32)] * 2
    got = kernel_call(functools.partial(begin_body, lay.near, lay.nd), out, info, (past, operator, incident), (), scratch)
    return got[: len(owners)], got[len(owners)], got[len(owners) + 1 :]


def join_body(near, waves, loose, info, *refs):
    ins, taken, out = refs[loose : len(refs) - 1 - waves], refs[len(refs) - 1 - waves : -1], refs[-1]
    per, rows = len(ins) // near, ins[0].shape[0]
    for kn in range(near):
        value = total_of(ins[kn * per : (kn + 1) * per])
        if waves:
            value = value - info[0].astype(F32) * jnp.concatenate([wave[...].astype(F32) for wave in taken], 0)
        out[pl.ds(kn * rows, rows), :] = value.astype(BF16)


def join(lay, groups, loose=(), waves=()):
    rows, columns = groups[0][0].shape
    out = jax.ShapeDtypeStruct((rows * len(groups), columns), BF16)
    body = functools.partial(join_body, len(groups), len(waves))
    info = [(lay.z == 0).astype(jnp.int32)]
    return kernel_call(body, out, info, [b for g in groups for b in g] + list(waves), loose)


def invert_body(near, loose, info, *refs):
    parts, operators, out = refs[loose : -1 - near], refs[-1 - near : -1], refs[-1]
    rhs = (-total_of(parts)).astype(BF16)
    rows = rhs.shape[0] // near
    out[...] = tree_sum(
        [times_transposed(rhs[k * rows : (k + 1) * rows], op[...]) for k, op in enumerate(operators)]
    ).astype(BF16)


def invert(lay, parts, operators, loose=()):
    out = jax.ShapeDtypeStruct((parts[0].shape[0] // lay.near, operators[0].shape[0]), BF16)
    return kernel_call(functools.partial(invert_body, lay.near), out, [lay.d], (*parts, *operators), loose)


def apply_body(near, nd, loose, info, *refs):
    refs, (operand, value) = refs[loose:-2], refs[-2:]
    refs, outs = refs[: -1 - nd], refs[-1 - nd :]
    parts, past_ref, operators = refs[: -1 - near], refs[-1 - near], refs[-near:]
    current_ref, totals = outs[0], outs[1:]
    far = len(parts) // nd
    rows = parts[0].shape[0]
    for kd in range(nd):
        current_ref[pl.ds(kd * rows, rows), :] = total_of(parts[kd * far : (kd + 1) * far]).astype(BF16)

    @pl.when(info[0] == 0)
    def _():
        operand[...] = current_ref[...]

    @pl.when(info[0] != 0)
    def _():
        operand[...] = past_ref[...]

    for kn in range(near):
        value[...] = times_transposed(operand[...], operators[kn][...])
        for kd in range(nd):
            totals[kd][pl.ds(kn * rows, rows), :] = part_of(value, info[0] ^ kd, rows).astype(BF16)


def apply(lay, parts, past, operators):
    rows, columns = parts[0].shape
    out = [jax.ShapeDtypeStruct((rows * lay.nd, columns), BF16)]
    out += [jax.ShapeDtypeStruct((rows * lay.near, operators[0].shape[0]), BF16)] * lay.nd
    body = functools.partial(apply_body, lay.near, lay.nd)
    scratch = [pltpu.VMEM(past.shape, BF16), pltpu.VMEM((rows * lay.nd, operators[0].shape[0]), F32)]
    current, *totals = kernel_call(body, out, [lay.d], (*parts, past, *operators), (), scratch)
    return current, totals


def finish_body(steps, loose, info, *refs):
    ins, (out, hist, total) = refs[loose:-3], refs[-3:]
    per = len(ins) // steps
    pieces = info.shape[0] - 1
    rows = total.shape[0] // pieces
    each = ins[0].shape[0] // rows
    for step in range(steps):
        for k in range(pieces):
            start = pl.multiple_of(info[1 + k] * rows, rows)
            block = ins[step * per + k // each][pl.ds((k % each) * rows, rows), :]
            total[pl.ds(start, rows), :] = block.astype(F32)
        turned = total[...].T.astype(BF16)
        out[step] = turned

        @pl.when(info[0] == steps - 1 - step)
        def _():
            hist[0] = turned


def finish(lay, blocks):
    steps = len(blocks)
    columns, exc = blocks[0][0].shape[1], blocks[0][0].shape[0] * lay.near
    shapes = [jax.ShapeDtypeStruct((k, columns, exc), BF16) for k in (steps, 1)]
    flat = [b for g in blocks for b in g]
    info = [lay.d, *lay.owners()]
    return kernel_call(functools.partial(finish_body, steps), shapes, info, flat, (), [pltpu.VMEM((exc, columns), F32)])


def over_rows(lay, partial):
    return [
        lay.move(partial, kd=kd, kf=kf) if kd or kf else partial for kd in range(lay.nd) for kf in range(lay.far)
    ]


def over_near(lay, block):
    return [block] + [lay.move(block, kn=kn) for kn in range(1, lay.near)]


def along_col(lay, total):
    got = {kz: lay.move(total, kz=kz) for kz in reversed(range(1, lay.nc))}
    return [total] + [got[kz] for kz in range(1, lay.nc)]


def two_steps(excitation, delay_ops, inverse_op, history):
    lay = Layout()
    operator, stored = delay_ops[0], history[0]
    pieces, part, waves = begin(lay, stored, operator, excitation)
    got = [
        [lay.move(pieces[kn * lay.nd + kd], kd=kd, kn=kn) if kd or kn else pieces[0] for kd in range(lay.nd)]
        for kn in range(lay.near)
    ]
    inverse = over_near(lay, inverse_op)
    total = join(lay, got)
    past = from_behind(part, "delay", 1)
    waves = [lay.move(wave, kn=kn) if kn else wave for kn, wave in enumerate(waves)]
    direct = over_near(lay, operator)
    partial = invert(lay, along_col(lay, total), inverse, ())
    current, totals = apply(lay, over_rows(lay, partial), past, direct)
    total = join(lay, [[lay.move(block, kd=kd) if kd else block for kd, block in enumerate(totals)]], (), waves)
    partial = invert(lay, along_col(lay, total), inverse)
    across = over_rows(lay, partial)
    last = join(lay, [across[kd * lay.far : (kd + 1) * lay.far] for kd in range(lay.nd)])
    return tuple(finish(lay, [over_near(lay, current), over_near(lay, last)]))


def on_device(excitation, delay_ops, inverse_op, history):
    sizes = [lax.axis_size(axis) for axis in ("delay", "row", "col")]
    steps, _, exc = excitation.shape
    follows = range(1, steps)
    share = exc // (sizes[0] * 2)
    if all(n & (n - 1) == 0 and n > 1 for n in sizes) and len(follows) == 1 and share and share % TILE_ROWS == 0:
        return two_steps(excitation, delay_ops, inverse_op, history)
    return general(excitation, delay_ops, inverse_op, history)


def solution(mesh):
    in_specs = (
        P(None, "row", None),
        P("delay", "row", "col"),
        P("col", "row"),
        P("delay", "col", None),
    )
    out_specs = (P(None, "col", None), P("delay", "col", None))
    return jax.shard_map(
        on_device, mesh=mesh, in_specs=in_specs, out_specs=out_specs, check_vma=False
    )
```

```python
import functools

import jax
import jax.numpy as jnp
from jax import lax
from jax.experimental import pallas as pl
from jax.experimental.pallas import tpu as pltpu
from jax.sharding import PartitionSpec as P

F32 = jnp.float32
BF16 = jnp.bfloat16
TILE_ROWS = 16


def routes(axis):
    n = lax.axis_size(axis)
    if n & (n - 1) == 0:
        return [[(i, i ^ k) for i in range(n)] for k in range(1, n)]
    return [[(i, (i + k) % n) for i in range(n)] for k in range(1, n)]


def tree_sum(blocks):
    while len(blocks) > 1:
        pairs = [a + b for a, b in zip(blocks[::2], blocks[1::2])]
        blocks = pairs + ([blocks[-1]] if len(blocks) % 2 else [])
    return blocks[0]


def exchange_sum(block, axis):
    block = lax.optimization_barrier(block)
    blocks = [block] + [lax.ppermute(block, axis, route) for route in routes(axis)]
    return tree_sum([b.astype(F32) for b in blocks])


def piece(block, index, rows):
    return lax.dynamic_slice_in_dim(block, index * rows, rows, 0)


def scatter_sum(block, axis):
    n = lax.axis_size(axis)
    rows = block.shape[0] // n
    me = lax.axis_index(axis)
    parts = [piece(block, me, rows)]
    for route in routes(axis):
        target = jnp.array([t for _, t in route])[me]
        parts.append(lax.ppermute(piece(block, target, rows), axis, route))
    return tree_sum([p.astype(F32) for p in parts])


def gather(block, axis):
    n = lax.axis_size(axis)
    rows = block.shape[0]
    me = lax.axis_index(axis)
    whole = jnp.zeros((n * rows,) + block.shape[1:], block.dtype)
    whole = lax.dynamic_update_slice_in_dim(whole, block, me * rows, 0)
    for route in routes(axis):
        source = jnp.array([s for s, _ in sorted(route, key=lambda pair: pair[1])])[me]
        whole = lax.dynamic_update_slice_in_dim(whole, lax.ppermute(block, axis, route), source * rows, 0)
    return whole


def from_behind(block, axis, distance):
    n = lax.axis_size(axis)
    route = [(i - distance, i) for i in range(n) if i >= distance]
    return lax.ppermute(block, axis, route) if route else jnp.zeros_like(block)


def spread(block, axis, source):
    me = lax.axis_index(axis)
    out = block
    for target in range(lax.axis_size(axis)):
        if target != source:
            out = jnp.where(me == target, lax.ppermute(block, axis, [(source, target)]), out)
    return out


def times_transposed(a, b):
    return lax.dot_general(a, b, (((1,), (1,)), ((), ())), preferred_element_type=F32)


def general(excitation, delay_ops, inverse_op, history):
    steps, _, exc = excitation.shape
    operator, stored = delay_ops[0], history[0]
    nd = lax.axis_size("delay")
    me = lax.axis_index("delay")
    share = exc // nd
    stored_t = stored.T
    older = [scatter_sum(times_transposed(stored_t, operator).astype(BF16), "delay")]
    for step in range(1, steps):
        earlier = from_behind(stored_t, "delay", step)
        older.append(scatter_sum(times_transposed(earlier, operator).astype(BF16), "delay"))
    shortest = [spread(operator, "delay", lag) for lag in range(min(steps - 1, nd))]
    incident = [piece(excitation[step].T, me, share).astype(F32) for step in range(steps)]
    produced = []
    for step in range(steps):
        total = older[step]
        for lag in range(min(step, nd)):
            total = total + times_transposed(produced[step - 1 - lag], shortest[lag])
        retarded = exchange_sum(total.astype(BF16), "col")
        rhs = (incident[step] - retarded).astype(BF16)
        current = exchange_sum(times_transposed(rhs, inverse_op).astype(BF16), "row").astype(BF16)
        produced.append(current)
    whole = [gather(current, "delay").T for current in produced]
    currents = jnp.stack(whole)
    newest_first = jnp.stack(whole[::-1])
    picked = lax.dynamic_index_in_dim(newest_first, jnp.clip(me, 0, steps - 1), 0, keepdims=False)
    if nd > steps:
        picked = jnp.where(me < steps, picked, from_behind(stored, "delay", steps))
    return currents, picked[None]


class Layout:
    def __init__(self):
        self.nd = lax.axis_size("delay")
        self.nr = lax.axis_size("row")
        self.nc = lax.axis_size("col")
        self.near = 2 if self.nr % 2 == 0 else 1
        self.far = self.nr // self.near
        self.d = lax.axis_index("delay")
        self.n = lax.axis_index("row") % self.near
        self.z = lax.axis_index("col")

    def move(self, block, kd=0, kf=0, kn=0, kz=0, only=None):
        pairs = []
        for d in range(self.nd) if only is None else only:
            for r in range(self.nr):
                for z in range(self.nc):
                    to = ((d ^ kd) * self.nr + (r ^ (kf * self.near + kn))) * self.nc + (z ^ kz)
                    pairs.append(((d * self.nr + r) * self.nc + z, to))
        return lax.ppermute(block, ("delay", "row", "col"), pairs)

    def owners(self):
        return [(self.n ^ kn) * self.nd + (self.d ^ kd) for kn in range(self.near) for kd in range(self.nd)]


def turned_about(body, loose, count, info, *refs):
    inputs = refs[loose : loose + count][::-1]
    body(loose, info, *refs[:loose], *inputs, *refs[loose + count :])


def kernel_call(body, out_shape, info, inputs, loose=(), scratch=()):
    vmem = pl.BlockSpec(memory_space=pltpu.VMEM)
    return pl.pallas_call(
        functools.partial(turned_about, body, len(loose), len(inputs)),
        out_shape=out_shape,
        in_specs=[pl.BlockSpec(memory_space=pltpu.SMEM)] + [pl.BlockSpec(memory_space=pl.ANY)] * len(loose) + [vmem] * len(inputs),
        out_specs=jax.tree.map(lambda _: vmem, out_shape),
        scratch_shapes=list(scratch),
        compiler_params=pltpu.CompilerParams(vmem_limit_bytes=8 << 20),
    )(jnp.stack(info), *loose, *inputs[::-1])


def total_of(refs):
    return tree_sum([ref[...].astype(F32) for ref in refs])


def part_of(ref, index, rows):
    return ref[pl.ds(pl.multiple_of(index * rows, rows), rows), :]


def begin_body(loose, info, total_ref, *pieces):
    for k, piece in enumerate(pieces):
        piece[...] = part_of(total_ref, info[k], piece.shape[0])


def begin(lay, past, operator):
    total = lax.dot_general(past, operator, (((0,), (1,)), ((), ())), preferred_element_type=F32).astype(BF16)
    owners = lay.owners()
    out = [jax.ShapeDtypeStruct((total.shape[0] // len(owners), total.shape[1]), BF16)] * len(owners)
    return kernel_call(begin_body, out, owners, (total,))


def part_body(loose, info, *refs):
    past_ref, part_ref, turned = refs[loose:]
    turned[...] = past_ref[...].astype(F32).T
    part_ref[...] = part_of(turned, info[0], part_ref.shape[0]).astype(BF16)


def part_cut(lay, past, after):
    columns, exc = past.shape
    out = jax.ShapeDtypeStruct((exc // lay.near, columns), BF16)
    return kernel_call(part_body, out, [lay.n], (past,), after, [pltpu.VMEM((exc, columns), F32)])


def wave_body(step, loose, info, *refs):
    incident_ref, outs, turned = refs[loose], refs[loose + 1 : -1], refs[-1]
    turned[...] = incident_ref[step].astype(F32).T
    for kn, out in enumerate(outs):
        out[...] = part_of(turned, info[kn], out.shape[0]).astype(BF16)


def wave_cut(lay, incident, step, after):
    rows, exc = incident.shape[1:]
    owners = lay.owners()[:: lay.nd]
    out = [jax.ShapeDtypeStruct((exc // (lay.near * lay.nd), rows), BF16)] * lay.near
    body = functools.partial(wave_body, step)
    return kernel_call(body, out, owners, (incident,), after, [pltpu.VMEM((exc, rows), F32)])


def join_body(near, loose, info, *refs):
    ins, out = refs[loose:-1], refs[-1]
    per, rows = len(ins) // near, ins[0].shape[0]
    for kn in range(near):
        out[pl.ds(kn * rows, rows), :] = total_of(ins[kn * per : (kn + 1) * per]).astype(BF16)


def join(lay, groups, loose=()):
    rows, columns = groups[0][0].shape
    out = jax.ShapeDtypeStruct((rows * len(groups), columns), BF16)
    return kernel_call(functools.partial(join_body, len(groups)), out, [lay.d], [b for g in groups for b in g], loose)


def invert_body(near, loose, info, *refs):
    refs, out = refs[loose:-1], refs[-1]
    parts, waves, operators = refs[: -2 * near], refs[-2 * near : -near], refs[-near:]
    retarded = total_of(parts)
    rows = retarded.shape[0] // near
    terms = []
    for kn in range(near):
        rhs = (waves[kn][...].astype(F32) - retarded[kn * rows : (kn + 1) * rows]).astype(BF16)
        terms.append(times_transposed(rhs, operators[kn][...]))
    out[...] = tree_sum(terms).astype(BF16)


def invert(lay, parts, waves, operators, loose=()):
    out = jax.ShapeDtypeStruct((parts[0].shape[0] // lay.near, operators[0].shape[0]), BF16)
    body = functools.partial(invert_body, lay.near)
    return kernel_call(body, out, [lay.d], (*parts, *waves, *operators), loose)


def apply_body(near, nd, loose, info, *refs):
    refs, (operand, value) = refs[loose:-2], refs[-2:]
    refs, outs = refs[: -1 - nd], refs[-1 - nd :]
    parts, past_ref, operators = refs[: -1 - near], refs[-1 - near], refs[-near:]
    current_ref, totals = outs[0], outs[1:]
    far = len(parts) // nd
    rows = parts[0].shape[0]
    for kd in range(nd):
        current_ref[pl.ds(kd * rows, rows), :] = total_of(parts[kd * far : (kd + 1) * far]).astype(BF16)

    @pl.when(info[0] == 0)
    def _():
        operand[...] = current_ref[...]

    @pl.when(info[0] != 0)
    def _():
        operand[...] = past_ref[...]

    for kn in range(near):
        value[...] = times_transposed(operand[...], operators[kn][...])
        for kd in range(nd):
            totals[kd][pl.ds(kn * rows, rows), :] = part_of(value, info[0] ^ kd, rows).astype(BF16)


def apply(lay, parts, past, operators):
    rows, columns = parts[0].shape
    out = [jax.ShapeDtypeStruct((rows * lay.nd, columns), BF16)]
    out += [jax.ShapeDtypeStruct((rows * lay.near, operators[0].shape[0]), BF16)] * lay.nd
    body = functools.partial(apply_body, lay.near, lay.nd)
    scratch = [pltpu.VMEM(past.shape, BF16), pltpu.VMEM((rows * lay.nd, operators[0].shape[0]), F32)]
    current, *totals = kernel_call(body, out, [lay.d], (*parts, past, *operators), (), scratch)
    return current, totals


def place(info, blocks, total):
    pieces = info.shape[0] - 1
    rows = total.shape[0] // pieces
    each = blocks[0].shape[0] // rows
    for k in range(pieces):
        start = pl.multiple_of(info[1 + k] * rows, rows)
        total[pl.ds(start, rows), :] = blocks[k // each][pl.ds((k % each) * rows, rows), :].astype(F32)
    return total[...].T.astype(BF16)


def turn_body(loose, info, *refs):
    refs[-2][...] = place(info, refs[loose:-2], refs[-1])


def turn(lay, blocks):
    columns, exc = blocks[0].shape[1], blocks[0].shape[0] * lay.near
    out = jax.ShapeDtypeStruct((columns, exc), BF16)
    return kernel_call(turn_body, out, [lay.d, *lay.owners()], blocks, (), [pltpu.VMEM((exc, columns), F32)])


def finish_body(done, info, *refs):
    earlier, blocks, (out, hist, total, turned, sems) = refs[:done], refs[done:-5], refs[-5:]

    def store(step, source):
        kept = pltpu.make_async_copy(source, hist.at[0], sems.at[done + 1])

        @pl.when(info[0] == done - step)
        def _():
            kept.start()

        copy = pltpu.make_async_copy(source, out.at[step], sems.at[step])
        copy.start()
        return copy, kept

    copies = [store(step, source) for step, source in enumerate(earlier)]
    turned[...] = place(info, blocks, total)
    copies.append(store(done, turned))
    for copy, _ in copies:
        copy.wait()
    copies[-1][1].wait()


def finish(lay, earlier, blocks):
    done = len(earlier)
    columns, exc = earlier[0].shape
    hbm, vmem = pl.BlockSpec(memory_space=pltpu.HBM), pl.BlockSpec(memory_space=pltpu.VMEM)
    return pl.pallas_call(
        functools.partial(finish_body, done),
        out_shape=[jax.ShapeDtypeStruct((k, columns, exc), BF16) for k in (done + 1, 1)],
        in_specs=[pl.BlockSpec(memory_space=pltpu.SMEM)] + [vmem] * (done + len(blocks)),
        out_specs=[hbm] * 2,
        scratch_shapes=[pltpu.VMEM((exc, columns), F32), pltpu.VMEM((columns, exc), BF16), pltpu.SemaphoreType.DMA((done + 2,))],
        compiler_params=pltpu.CompilerParams(vmem_limit_bytes=8 << 20),
    )(jnp.stack([lay.d, *lay.owners()]), *earlier, *blocks)


def over_rows(lay, partial):
    return [
        lay.move(partial, kd=kd, kf=kf) if kd or kf else partial for kd in range(lay.nd) for kf in range(lay.far)
    ]


def over_near(lay, block):
    return [block] + [lay.move(block, kn=kn) for kn in range(1, lay.near)]


def along_col(lay, total):
    got = {kz: lay.move(total, kz=kz) for kz in reversed(range(1, lay.nc))}
    return [total] + [got[kz] for kz in range(1, lay.nc)]


def from_cores(lay, pieces):
    return [lay.move(piece, kn=kn) if kn else piece for kn, piece in enumerate(pieces)]


def two_steps(excitation, delay_ops, inverse_op, history):
    lay = Layout()
    operator, stored = delay_ops[0], history[0]
    pieces = begin(lay, stored, operator)
    part = part_cut(lay, stored, (pieces[0],))
    got = [
        [lay.move(pieces[kn * lay.nd + kd], kd=kd, kn=kn) if kd or kn else pieces[0] for kd in range(lay.nd)]
        for kn in range(lay.near)
    ]
    cuts = wave_cut(lay, excitation, 0, (pieces[0],))
    inverse = over_near(lay, inverse_op)
    total = join(lay, got, (*cuts, part))
    past = from_behind(part, "delay", 1)
    direct = over_near(lay, operator)
    partial = invert(lay, along_col(lay, total), from_cores(lay, cuts), inverse)
    current, totals = apply(lay, over_rows(lay, partial), past, direct)
    cuts = wave_cut(lay, excitation, 1, (totals[0],))
    total = join(lay, [[lay.move(block, kd=kd) if kd else block for kd, block in enumerate(totals)]], cuts)
    turned = turn(lay, over_near(lay, current))
    partial = invert(lay, along_col(lay, total), from_cores(lay, cuts), inverse, ())
    across = over_rows(lay, partial)
    last = join(lay, [across[kd * lay.far : (kd + 1) * lay.far] for kd in range(lay.nd)])
    return tuple(finish(lay, [turned], over_near(lay, last)))


def on_device(excitation, delay_ops, inverse_op, history):
    sizes = [lax.axis_size(axis) for axis in ("delay", "row", "col")]
    steps, _, exc = excitation.shape
    follows = range(1, steps)
    share = exc // (sizes[0] * 2)
    if all(n & (n - 1) == 0 and n > 1 for n in sizes) and len(follows) == 1 and sizes[0] <= steps and share and share % TILE_ROWS == 0:
        return two_steps(excitation, delay_ops, inverse_op, history)
    return general(excitation, delay_ops, inverse_op, history)


def solution(mesh):
    in_specs = (
        P(None, "row", None),
        P("delay", "row", "col"),
        P("col", "row"),
        P("delay", "col", None),
    )
    out_specs = (P(None, "col", None), P("delay", "col", None))
    return jax.shard_map(
        on_device, mesh=mesh, in_specs=in_specs, out_specs=out_specs, check_vma=False
    )
```

```python
import functools

import jax
import jax.numpy as jnp
from jax import lax
from jax.experimental import pallas as pl
from jax.experimental.pallas import tpu as pltpu
from jax.sharding import PartitionSpec as P

F32 = jnp.float32
BF16 = jnp.bfloat16
TILE_ROWS = 16


def routes(axis):
    n = lax.axis_size(axis)
    if n & (n - 1) == 0:
        return [[(i, i ^ k) for i in range(n)] for k in range(1, n)]
    return [[(i, (i + k) % n) for i in range(n)] for k in range(1, n)]


def tree_sum(blocks):
    while len(blocks) > 1:
        pairs = [a + b for a, b in zip(blocks[::2], blocks[1::2])]
        blocks = pairs + ([blocks[-1]] if len(blocks) % 2 else [])
    return blocks[0]


def exchange_sum(block, axis):
    block = lax.optimization_barrier(block)
    blocks = [block] + [lax.ppermute(block, axis, route) for route in routes(axis)]
    return tree_sum([b.astype(F32) for b in blocks])


def piece(block, index, rows):
    return lax.dynamic_slice_in_dim(block, index * rows, rows, 0)


def scatter_sum(block, axis):
    n = lax.axis_size(axis)
    rows = block.shape[0] // n
    me = lax.axis_index(axis)
    parts = [piece(block, me, rows)]
    for route in routes(axis):
        target = jnp.array([t for _, t in route])[me]
        parts.append(lax.ppermute(piece(block, target, rows), axis, route))
    return tree_sum([p.astype(F32) for p in parts])


def gather(block, axis):
    n = lax.axis_size(axis)
    rows = block.shape[0]
    me = lax.axis_index(axis)
    whole = jnp.zeros((n * rows,) + block.shape[1:], block.dtype)
    whole = lax.dynamic_update_slice_in_dim(whole, block, me * rows, 0)
    for route in routes(axis):
        source = jnp.array([s for s, _ in sorted(route, key=lambda pair: pair[1])])[me]
        whole = lax.dynamic_update_slice_in_dim(whole, lax.ppermute(block, axis, route), source * rows, 0)
    return whole


def from_behind(block, axis, distance):
    n = lax.axis_size(axis)
    route = [(i - distance, i) for i in range(n) if i >= distance]
    return lax.ppermute(block, axis, route) if route else jnp.zeros_like(block)


def spread(block, axis, source):
    me = lax.axis_index(axis)
    out = block
    for target in range(lax.axis_size(axis)):
        if target != source:
            out = jnp.where(me == target, lax.ppermute(block, axis, [(source, target)]), out)
    return out


def times_transposed(a, b):
    return lax.dot_general(a, b, (((1,), (1,)), ((), ())), preferred_element_type=F32)


def general(excitation, delay_ops, inverse_op, history):
    steps, _, exc = excitation.shape
    operator, stored = delay_ops[0], history[0]
    nd = lax.axis_size("delay")
    me = lax.axis_index("delay")
    share = exc // nd
    stored_t = stored.T
    older = [scatter_sum(times_transposed(stored_t, operator).astype(BF16), "delay")]
    for step in range(1, steps):
        earlier = from_behind(stored_t, "delay", step)
        older.append(scatter_sum(times_transposed(earlier, operator).astype(BF16), "delay"))
    shortest = [spread(operator, "delay", lag) for lag in range(min(steps - 1, nd))]
    incident = [piece(excitation[step].T, me, share).astype(F32) for step in range(steps)]
    produced = []
    for step in range(steps):
        total = older[step]
        for lag in range(min(step, nd)):
            total = total + times_transposed(produced[step - 1 - lag], shortest[lag])
        retarded = exchange_sum(total.astype(BF16), "col")
        rhs = (incident[step] - retarded).astype(BF16)
        current = exchange_sum(times_transposed(rhs, inverse_op).astype(BF16), "row").astype(BF16)
        produced.append(current)
    whole = [gather(current, "delay").T for current in produced]
    currents = jnp.stack(whole)
    newest_first = jnp.stack(whole[::-1])
    picked = lax.dynamic_index_in_dim(newest_first, jnp.clip(me, 0, steps - 1), 0, keepdims=False)
    if nd > steps:
        picked = jnp.where(me < steps, picked, from_behind(stored, "delay", steps))
    return currents, picked[None]


class Layout:
    def __init__(self):
        self.nd = lax.axis_size("delay")
        self.nr = lax.axis_size("row")
        self.nc = lax.axis_size("col")
        self.near = 2 if self.nr % 2 == 0 else 1
        self.far = self.nr // self.near
        self.d = lax.axis_index("delay")
        self.n = lax.axis_index("row") % self.near
        self.z = lax.axis_index("col")

    def move(self, block, kd=0, kf=0, kn=0, kz=0, only=None):
        pairs = []
        for d in range(self.nd) if only is None else only:
            for r in range(self.nr):
                for z in range(self.nc):
                    to = ((d ^ kd) * self.nr + (r ^ (kf * self.near + kn))) * self.nc + (z ^ kz)
                    pairs.append(((d * self.nr + r) * self.nc + z, to))
        return lax.ppermute(block, ("delay", "row", "col"), pairs)


def farthest_first(body, numbers, loose, count, *refs):
    info, refs = [ref[0] for ref in refs[:numbers]], refs[numbers:]
    inputs = refs[loose : loose + count][::-1]
    body(loose, info, *refs[:loose], *inputs, *refs[loose + count :])


def kernel_call(body, out_shape, info, inputs, loose=(), scratch=()):
    vmem, smem = pl.BlockSpec(memory_space=pltpu.VMEM), pl.BlockSpec(memory_space=pltpu.SMEM)
    return pl.pallas_call(
        functools.partial(farthest_first, body, len(info), len(loose), len(inputs)),
        out_shape=out_shape,
        in_specs=[smem] * len(info) + [pl.BlockSpec(memory_space=pl.ANY)] * len(loose) + [vmem] * len(inputs),
        out_specs=jax.tree.map(lambda _: vmem, out_shape),
        scratch_shapes=list(scratch),
        compiler_params=pltpu.CompilerParams(vmem_limit_bytes=8 << 20),
    )(*[jnp.reshape(number, (1,)) for number in info], *loose, *inputs[::-1])


def owner(info, nd, k):
    return (info[1] ^ (k // nd)) * nd + (info[0] ^ (k % nd))


def total_of(refs):
    return tree_sum([ref[...].astype(F32) for ref in refs])


def part_of(ref, index, rows):
    return ref[pl.ds(pl.multiple_of(index * rows, rows), rows), :]


def begin_body(nd, loose, info, total_ref, *pieces):
    for k, piece in enumerate(pieces):
        piece[...] = part_of(total_ref, owner(info, nd, k), piece.shape[0])


def begin(lay, past, operator):
    total = lax.dot_general(past, operator, (((0,), (1,)), ((), ())), preferred_element_type=F32).astype(BF16)
    count = lay.near * lay.nd
    out = [jax.ShapeDtypeStruct((total.shape[0] // count, total.shape[1]), BF16)] * count
    return kernel_call(functools.partial(begin_body, lay.nd), out, [lay.d, lay.n], (total,))


def part_body(loose, info, *refs):
    past_ref, part_ref, turned = refs[loose:]
    turned[...] = past_ref[...].astype(F32).T
    part_ref[...] = part_of(turned, info[0], part_ref.shape[0]).astype(BF16)


def part_cut(lay, past, after):
    columns, exc = past.shape
    out = jax.ShapeDtypeStruct((exc // lay.near, columns), BF16)
    return kernel_call(part_body, out, [lay.n], (past,), after, [pltpu.VMEM((exc, columns), F32)])


def wave_body(step, nd, loose, info, *refs):
    incident_ref, outs, turned = refs[loose], refs[loose + 1 : -1], refs[-1]
    turned[...] = incident_ref[step].astype(F32).T
    for kn, out in enumerate(outs):
        out[...] = part_of(turned, owner(info, nd, kn * nd), out.shape[0]).astype(BF16)


def wave_cut(lay, incident, step, after):
    rows, exc = incident.shape[1:]
    out = [jax.ShapeDtypeStruct((exc // (lay.near * lay.nd), rows), BF16)] * lay.near
    body = functools.partial(wave_body, step, lay.nd)
    return kernel_call(body, out, [lay.d, lay.n], (incident,), after, [pltpu.VMEM((exc, rows), F32)])


def join_body(count, loose, info, *refs):
    ins, out = refs[loose:-1], refs[-1]
    rows = ins[0].shape[0]
    for k in range(count):
        out[pl.ds(k * rows, rows), :] = total_of(ins[k::count]).astype(BF16)


def join(lay, groups, loose=()):
    rows, columns = groups[0][0].shape
    out = jax.ShapeDtypeStruct((rows * len(groups), columns), BF16)
    flat = [block for blocks in zip(*groups) for block in blocks]
    return kernel_call(functools.partial(join_body, len(groups)), out, [lay.d], flat, loose)


def invert_body(near, loose, info, *refs):
    refs, out = refs[loose:-1], refs[-1]
    parts, waves, operators = refs[: -2 * near], refs[-2 * near : -near], refs[-near:]
    retarded = total_of(parts)
    rows = retarded.shape[0] // near
    terms = []
    for kn in range(near):
        rhs = (waves[kn][...].astype(F32) - retarded[kn * rows : (kn + 1) * rows]).astype(BF16)
        terms.append(times_transposed(rhs, operators[kn][...]))
    out[...] = tree_sum(terms).astype(BF16)


def invert(lay, parts, waves, operators, loose=()):
    out = jax.ShapeDtypeStruct((parts[0].shape[0] // lay.near, operators[0].shape[0]), BF16)
    body = functools.partial(invert_body, lay.near)
    return kernel_call(body, out, [lay.d], (*parts, *waves, *operators), loose)


def apply_body(near, nd, loose, info, *refs):
    refs, (operand, value) = refs[loose:-2], refs[-2:]
    refs, outs = refs[: -1 - nd], refs[-1 - nd :]
    parts, past_ref, operators = refs[: -1 - near], refs[-1 - near], refs[-near:]
    current_ref, totals = outs[0], outs[1:]
    rows = parts[0].shape[0]
    for kd in range(nd):
        current_ref[pl.ds(kd * rows, rows), :] = total_of(parts[kd::nd]).astype(BF16)

    @pl.when(info[0] == 0)
    def _():
        operand[...] = current_ref[...]

    @pl.when(info[0] != 0)
    def _():
        operand[...] = past_ref[...]

    for kn in range(near):
        value[...] = times_transposed(operand[...], operators[kn][...])
        for kd in range(nd):
            totals[kd][pl.ds(kn * rows, rows), :] = part_of(value, info[0] ^ kd, rows).astype(BF16)


def apply(lay, parts, past, operators):
    rows, columns = parts[0].shape
    out = [jax.ShapeDtypeStruct((rows * lay.nd, columns), BF16)]
    out += [jax.ShapeDtypeStruct((rows * lay.near, operators[0].shape[0]), BF16)] * lay.nd
    body = functools.partial(apply_body, lay.near, lay.nd)
    scratch = [pltpu.VMEM(past.shape, BF16), pltpu.VMEM((rows * lay.nd, operators[0].shape[0]), F32)]
    current, *totals = kernel_call(body, out, [lay.d], (*parts, past, *operators), (), scratch)
    return current, totals


def place(info, nd, blocks, total):
    rows = blocks[0].shape[0] // nd
    for k in range(total.shape[0] // rows):
        start = pl.multiple_of(owner(info, nd, k) * rows, rows)
        total[pl.ds(start, rows), :] = blocks[k // nd][pl.ds((k % nd) * rows, rows), :].astype(F32)
    return total[...].T.astype(BF16)


def turn_body(nd, loose, info, *refs):
    refs[-2][...] = place(info, nd, refs[loose:-2], refs[-1])


def turn(lay, blocks):
    columns, exc = blocks[0].shape[1], blocks[0].shape[0] * lay.near
    out = jax.ShapeDtypeStruct((columns, exc), BF16)
    scratch = [pltpu.VMEM((exc, columns), F32)]
    return kernel_call(functools.partial(turn_body, lay.nd), out, [lay.d, lay.n], blocks, (), scratch)


def finish_body(done, nd, d_ref, n_ref, *refs):
    info = [d_ref[0], n_ref[0]]
    earlier, blocks, (out, hist, total, turned, sems) = refs[:done], refs[done:-5], refs[-5:]

    def store(step, source):
        kept = pltpu.make_async_copy(source, hist.at[0], sems.at[done + 1])

        @pl.when(info[0] == done - step)
        def _():
            kept.start()

        copy = pltpu.make_async_copy(source, out.at[step], sems.at[step])
        copy.start()
        return copy, kept

    copies = [store(step, source) for step, source in enumerate(earlier)]
    turned[...] = place(info, nd, blocks, total)
    copies.append(store(done, turned))
    for copy, _ in copies:
        copy.wait()
    copies[-1][1].wait()


def finish(lay, earlier, blocks):
    done = len(earlier)
    columns, exc = earlier[0].shape
    hbm, vmem, smem = [pl.BlockSpec(memory_space=space) for space in (pltpu.HBM, pltpu.VMEM, pltpu.SMEM)]
    scratch = [pltpu.VMEM((exc, columns), F32), pltpu.VMEM((columns, exc), BF16), pltpu.SemaphoreType.DMA((done + 2,))]
    return pl.pallas_call(
        functools.partial(finish_body, done, lay.nd),
        out_shape=[jax.ShapeDtypeStruct((k, columns, exc), BF16) for k in (done + 1, 1)],
        in_specs=[smem] * 2 + [vmem] * (done + len(blocks)),
        out_specs=[hbm] * 2,
        scratch_shapes=scratch,
        compiler_params=pltpu.CompilerParams(vmem_limit_bytes=8 << 20),
    )(jnp.reshape(lay.d, (1,)), jnp.reshape(lay.n, (1,)), *earlier, *blocks)


def over_rows(lay, partial):
    return [
        lay.move(partial, kd=kd, kf=kf) if kd or kf else partial for kf in range(lay.far) for kd in range(lay.nd)
    ]


def over_near(lay, block):
    return [block] + [lay.move(block, kn=kn) for kn in range(1, lay.near)]


def along_col(lay, total):
    got = {kz: lay.move(total, kz=kz) for kz in reversed(range(1, lay.nc))}
    return [total] + [got[kz] for kz in range(1, lay.nc)]


def from_cores(lay, pieces):
    return [lay.move(piece, kn=kn) if kn else piece for kn, piece in enumerate(pieces)]


def two_steps(excitation, delay_ops, inverse_op, history):
    lay = Layout()
    operator, stored = delay_ops[0], history[0]
    pieces = begin(lay, stored, operator)
    part = part_cut(lay, stored, (pieces[0],))
    got = [
        [lay.move(pieces[kn * lay.nd + kd], kd=kd, kn=kn) if kd or kn else pieces[0] for kd in range(lay.nd)]
        for kn in range(lay.near)
    ]
    cuts = wave_cut(lay, excitation, 0, (pieces[0],))
    inverse = over_near(lay, inverse_op)
    total = join(lay, got, (*cuts, part))
    past = from_behind(part, "delay", 1)
    direct = over_near(lay, operator)
    partial = invert(lay, along_col(lay, total), from_cores(lay, cuts), inverse)
    current, totals = apply(lay, over_rows(lay, partial), past, direct)
    cuts = wave_cut(lay, excitation, 1, (totals[0],))
    total = join(lay, [[lay.move(block, kd=kd) if kd else block for kd, block in enumerate(totals)]], cuts)
    turned = turn(lay, over_near(lay, current))
    partial = invert(lay, along_col(lay, total), from_cores(lay, cuts), inverse, ())
    across = over_rows(lay, partial)
    last = join(lay, [across[kd :: lay.nd] for kd in range(lay.nd)])
    return tuple(finish(lay, [turned], over_near(lay, last)))


def on_device(excitation, delay_ops, inverse_op, history):
    sizes = [lax.axis_size(axis) for axis in ("delay", "row", "col")]
    steps, _, exc = excitation.shape
    follows = range(1, steps)
    share = exc // (sizes[0] * 2)
    if all(n & (n - 1) == 0 and n > 1 for n in sizes) and len(follows) == 1 and sizes[0] <= steps and share and share % TILE_ROWS == 0:
        return two_steps(excitation, delay_ops, inverse_op, history)
    return general(excitation, delay_ops, inverse_op, history)


def solution(mesh):
    in_specs = (
        P(None, "row", None),
        P("delay", "row", "col"),
        P("col", "row"),
        P("delay", "col", None),
    )
    out_specs = (P(None, "col", None), P("delay", "col", None))
    return jax.shard_map(
        on_device, mesh=mesh, in_specs=in_specs, out_specs=out_specs, check_vma=False
    )
```

```python
import functools

import jax
import jax.numpy as jnp
from jax import lax
from jax.experimental import pallas as pl
from jax.experimental.pallas import tpu as pltpu
from jax.sharding import PartitionSpec as P

F32 = jnp.float32
BF16 = jnp.bfloat16
TILE_ROWS = 16


def routes(axis):
    n = lax.axis_size(axis)
    if n & (n - 1) == 0:
        return [[(i, i ^ k) for i in range(n)] for k in range(1, n)]
    return [[(i, (i + k) % n) for i in range(n)] for k in range(1, n)]


def tree_sum(blocks):
    while len(blocks) > 1:
        pairs = [a + b for a, b in zip(blocks[::2], blocks[1::2])]
        blocks = pairs + ([blocks[-1]] if len(blocks) % 2 else [])
    return blocks[0]


def exchange_sum(block, axis):
    block = lax.optimization_barrier(block)
    blocks = [block] + [lax.ppermute(block, axis, route) for route in routes(axis)]
    return tree_sum([b.astype(F32) for b in blocks])


def piece(block, index, rows):
    return lax.dynamic_slice_in_dim(block, index * rows, rows, 0)


def scatter_sum(block, axis):
    n = lax.axis_size(axis)
    rows = block.shape[0] // n
    me = lax.axis_index(axis)
    parts = [piece(block, me, rows)]
    for route in routes(axis):
        target = jnp.array([t for _, t in route])[me]
        parts.append(lax.ppermute(piece(block, target, rows), axis, route))
    return tree_sum([p.astype(F32) for p in parts])


def gather(block, axis):
    n = lax.axis_size(axis)
    rows = block.shape[0]
    me = lax.axis_index(axis)
    whole = jnp.zeros((n * rows,) + block.shape[1:], block.dtype)
    whole = lax.dynamic_update_slice_in_dim(whole, block, me * rows, 0)
    for route in routes(axis):
        source = jnp.array([s for s, _ in sorted(route, key=lambda pair: pair[1])])[me]
        whole = lax.dynamic_update_slice_in_dim(whole, lax.ppermute(block, axis, route), source * rows, 0)
    return whole


def from_behind(block, axis, distance):
    n = lax.axis_size(axis)
    route = [(i - distance, i) for i in range(n) if i >= distance]
    return lax.ppermute(block, axis, route) if route else jnp.zeros_like(block)


def spread(block, axis, source):
    me = lax.axis_index(axis)
    out = block
    for target in range(lax.axis_size(axis)):
        if target != source:
            out = jnp.where(me == target, lax.ppermute(block, axis, [(source, target)]), out)
    return out


def times_transposed(a, b):
    return lax.dot_general(a, b, (((1,), (1,)), ((), ())), preferred_element_type=F32)


def general(excitation, delay_ops, inverse_op, history):
    steps, _, exc = excitation.shape
    operator, stored = delay_ops[0], history[0]
    nd = lax.axis_size("delay")
    me = lax.axis_index("delay")
    share = exc // nd
    stored_t = stored.T
    older = [scatter_sum(times_transposed(stored_t, operator).astype(BF16), "delay")]
    for step in range(1, steps):
        earlier = from_behind(stored_t, "delay", step)
        older.append(scatter_sum(times_transposed(earlier, operator).astype(BF16), "delay"))
    shortest = [spread(operator, "delay", lag) for lag in range(min(steps - 1, nd))]
    incident = [piece(excitation[step].T, me, share).astype(F32) for step in range(steps)]
    produced = []
    for step in range(steps):
        total = older[step]
        for lag in range(min(step, nd)):
            total = total + times_transposed(produced[step - 1 - lag], shortest[lag])
        retarded = exchange_sum(total.astype(BF16), "col")
        rhs = (incident[step] - retarded).astype(BF16)
        current = exchange_sum(times_transposed(rhs, inverse_op).astype(BF16), "row").astype(BF16)
        produced.append(current)
    whole = [gather(current, "delay").T for current in produced]
    currents = jnp.stack(whole)
    newest_first = jnp.stack(whole[::-1])
    picked = lax.dynamic_index_in_dim(newest_first, jnp.clip(me, 0, steps - 1), 0, keepdims=False)
    if nd > steps:
        picked = jnp.where(me < steps, picked, from_behind(stored, "delay", steps))
    return currents, picked[None]


class Layout:
    def __init__(self):
        self.nd = lax.axis_size("delay")
        self.nr = lax.axis_size("row")
        self.nc = lax.axis_size("col")
        self.near = 2 if self.nr % 2 == 0 else 1
        self.far = self.nr // self.near
        self.d = lax.axis_index("delay")
        self.n = lax.axis_index("row") % self.near
        self.z = lax.axis_index("col")

    def move(self, block, kd=0, kf=0, kn=0, kz=0, only=None):
        pairs = []
        for d in range(self.nd) if only is None else only:
            for r in range(self.nr):
                for z in range(self.nc):
                    to = ((d ^ kd) * self.nr + (r ^ (kf * self.near + kn))) * self.nc + (z ^ kz)
                    pairs.append(((d * self.nr + r) * self.nc + z, to))
        return lax.ppermute(block, ("delay", "row", "col"), pairs)


def farthest_first(body, numbers, loose, count, *refs):
    info, refs = [ref[0] for ref in refs[:numbers]], refs[numbers:]
    inputs = refs[loose : loose + count][::-1]
    body(loose, info, *refs[:loose], *inputs, *refs[loose + count :])


def kernel_call(body, out_shape, info, inputs, loose=(), scratch=()):
    vmem, smem = pl.BlockSpec(memory_space=pltpu.VMEM), pl.BlockSpec(memory_space=pltpu.SMEM)
    return pl.pallas_call(
        functools.partial(farthest_first, body, len(info), len(loose), len(inputs)),
        out_shape=out_shape,
        in_specs=[smem] * len(info) + [pl.BlockSpec(memory_space=pl.ANY)] * len(loose) + [vmem] * len(inputs),
        out_specs=jax.tree.map(lambda _: vmem, out_shape),
        scratch_shapes=list(scratch),
        compiler_params=pltpu.CompilerParams(vmem_limit_bytes=8 << 20),
    )(*[jnp.reshape(number, (1,)) for number in info], *loose, *inputs[::-1])


def owner(info, nd, k):
    return (info[1] ^ (k // nd)) * nd + (info[0] ^ (k % nd))


def total_of(refs):
    return tree_sum([ref[...].astype(F32) for ref in refs])


def part_of(ref, index, rows):
    return ref[pl.ds(pl.multiple_of(index * rows, rows), rows), :]


def begin_body(nd, loose, info, total_ref, *pieces):
    for k, piece in enumerate(pieces):
        piece[...] = part_of(total_ref, owner(info, nd, k), piece.shape[0])


def begin(lay, past, operator):
    total = lax.dot_general(past, operator, (((0,), (1,)), ((), ())), preferred_element_type=F32).astype(BF16)
    count = lay.near * lay.nd
    out = [jax.ShapeDtypeStruct((total.shape[0] // count, total.shape[1]), BF16)] * count
    return kernel_call(functools.partial(begin_body, lay.nd), out, [lay.d, lay.n], (total,))


def part_body(loose, info, *refs):
    past_ref, part_ref, turned = refs[loose:]
    turned[...] = past_ref[...].astype(F32).T
    part_ref[...] = part_of(turned, info[0], part_ref.shape[0]).astype(BF16)


def part_cut(lay, past, after):
    columns, exc = past.shape
    out = jax.ShapeDtypeStruct((exc // lay.near, columns), BF16)
    return kernel_call(part_body, out, [lay.n], (past,), after, [pltpu.VMEM((exc, columns), F32)])


def wave_body(step, nd, loose, info, *refs):
    incident_ref, outs, turned = refs[loose], refs[loose + 1 : -1], refs[-1]
    turned[...] = incident_ref[step].astype(F32).T
    for kn, out in enumerate(outs):
        out[...] = part_of(turned, owner(info, nd, kn * nd), out.shape[0]).astype(BF16)


def wave_cut(lay, incident, step, after):
    rows, exc = incident.shape[1:]
    out = [jax.ShapeDtypeStruct((exc // (lay.near * lay.nd), rows), BF16)] * lay.near
    body = functools.partial(wave_body, step, lay.nd)
    return kernel_call(body, out, [lay.d, lay.n], (incident,), after, [pltpu.VMEM((exc, rows), F32)])


def join_body(count, loose, info, *refs):
    ins, out = refs[loose:-1], refs[-1]
    rows = ins[0].shape[0]
    for k in range(count):
        out[pl.ds(k * rows, rows), :] = total_of(ins[k::count]).astype(BF16)


def join(lay, groups, loose=()):
    rows, columns = groups[0][0].shape
    out = jax.ShapeDtypeStruct((rows * len(groups), columns), BF16)
    flat = [block for blocks in zip(*groups) for block in blocks]
    return kernel_call(functools.partial(join_body, len(groups)), out, [lay.d], flat, loose)


def invert_body(near, loose, info, *refs):
    refs, out = refs[loose:-1], refs[-1]
    parts, waves, operators = refs[: -2 * near], refs[-2 * near : -near], refs[-near:]
    retarded = total_of(parts)
    rows = retarded.shape[0] // near
    terms = []
    for kn in range(near):
        rhs = (waves[kn][...].astype(F32) - retarded[kn * rows : (kn + 1) * rows]).astype(BF16)
        terms.append(times_transposed(rhs, operators[kn][...]))
    out[...] = tree_sum(terms).astype(BF16)


def invert(lay, parts, waves, operators, loose=()):
    out = jax.ShapeDtypeStruct((parts[0].shape[0] // lay.near, operators[0].shape[0]), BF16)
    body = functools.partial(invert_body, lay.near)
    return kernel_call(body, out, [lay.d], (*parts, *waves, *operators), loose)


def apply_body(near, nd, loose, info, *refs):
    refs = refs[loose:]
    refs, (current_ref, operand, *totals) = refs[: -1 - nd], refs[-1 - nd :]
    parts, past_ref, operators = refs[: -1 - near], refs[-1 - near], refs[-near:]
    rows = parts[0].shape[0]
    for kd in range(nd):
        current_ref[pl.ds(kd * rows, rows), :] = total_of(parts[kd::nd]).astype(BF16)

    @pl.when(info[0] == 0)
    def _():
        operand[...] = current_ref[...]

    @pl.when(info[0] != 0)
    def _():
        operand[...] = past_ref[...]

    for kd, total in enumerate(totals, 1):
        wanted = part_of(operand, info[0] ^ kd, rows)
        for kn in range(near):
            total[pl.ds(kn * rows, rows), :] = times_transposed(wanted, operators[kn][...]).astype(BF16)


def own_body(near, loose, info, *refs):
    operand, operators, total = refs[loose], refs[loose + 1 : -1], refs[-1]
    rows = total.shape[0] // near
    wanted = part_of(operand, info[0], rows)
    for kn in range(near):
        total[pl.ds(kn * rows, rows), :] = times_transposed(wanted, operators[kn][...]).astype(BF16)


def apply(lay, parts, past, operators):
    rows, columns = parts[0].shape
    total = jax.ShapeDtypeStruct((rows * lay.near, operators[0].shape[0]), BF16)
    out = [jax.ShapeDtypeStruct((rows * lay.nd, columns), BF16)] * 2 + [total] * (lay.nd - 1)
    body = functools.partial(apply_body, lay.near, lay.nd)
    current, operand, *others = kernel_call(body, out, [lay.d], (*parts, past, *operators))
    own = kernel_call(functools.partial(own_body, lay.near), total, [lay.d], (operand, *operators))
    return current, [own, *others]


def place(info, nd, blocks, total):
    rows = blocks[0].shape[0] // nd
    for k in range(total.shape[0] // rows):
        start = pl.multiple_of(owner(info, nd, k) * rows, rows)
        total[pl.ds(start, rows), :] = blocks[k // nd][pl.ds((k % nd) * rows, rows), :].astype(F32)
    return total[...].T.astype(BF16)


def turn_body(nd, loose, info, *refs):
    refs[-2][...] = place(info, nd, refs[loose:-2], refs[-1])


def turn(lay, blocks):
    columns, exc = blocks[0].shape[1], blocks[0].shape[0] * lay.near
    out = jax.ShapeDtypeStruct((columns, exc), BF16)
    scratch = [pltpu.VMEM((exc, columns), F32)]
    return kernel_call(functools.partial(turn_body, lay.nd), out, [lay.d, lay.n], blocks, (), scratch)


def finish_body(done, nd, d_ref, n_ref, *refs):
    info = [d_ref[0], n_ref[0]]
    earlier, blocks, (out, hist, total, turned, sems) = refs[:done], refs[done:-5], refs[-5:]

    def store(step, source):
        kept = pltpu.make_async_copy(source, hist.at[0], sems.at[done + 1])

        @pl.when(info[0] == done - step)
        def _():
            kept.start()

        copy = pltpu.make_async_copy(source, out.at[step], sems.at[step])
        copy.start()
        return copy, kept

    copies = [store(step, source) for step, source in enumerate(earlier)]
    turned[...] = place(info, nd, blocks, total)
    copies.append(store(done, turned))
    for copy, _ in copies:
        copy.wait()
    copies[-1][1].wait()


def finish(lay, earlier, blocks):
    done = len(earlier)
    columns, exc = earlier[0].shape
    hbm, vmem, smem = [pl.BlockSpec(memory_space=space) for space in (pltpu.HBM, pltpu.VMEM, pltpu.SMEM)]
    scratch = [pltpu.VMEM((exc, columns), F32), pltpu.VMEM((columns, exc), BF16), pltpu.SemaphoreType.DMA((done + 2,))]
    return pl.pallas_call(
        functools.partial(finish_body, done, lay.nd),
        out_shape=[jax.ShapeDtypeStruct((k, columns, exc), BF16) for k in (done + 1, 1)],
        in_specs=[smem] * 2 + [vmem] * (done + len(blocks)),
        out_specs=[hbm] * 2,
        scratch_shapes=scratch,
        compiler_params=pltpu.CompilerParams(vmem_limit_bytes=8 << 20),
    )(jnp.reshape(lay.d, (1,)), jnp.reshape(lay.n, (1,)), *earlier, *blocks)


def over_rows(lay, partial):
    return [
        lay.move(partial, kd=kd, kf=kf) if kd or kf else partial for kf in range(lay.far) for kd in range(lay.nd)
    ]


def over_near(lay, block):
    return [block] + [lay.move(block, kn=kn) for kn in range(1, lay.near)]


def along_col(lay, total):
    got = {kz: lay.move(total, kz=kz) for kz in reversed(range(1, lay.nc))}
    return [total] + [got[kz] for kz in range(1, lay.nc)]


def from_cores(lay, pieces):
    return [lay.move(piece, kn=kn) if kn else piece for kn, piece in enumerate(pieces)]


def two_steps(excitation, delay_ops, inverse_op, history):
    lay = Layout()
    operator, stored = delay_ops[0], history[0]
    pieces = begin(lay, stored, operator)
    part = part_cut(lay, stored, (pieces[0],))
    got = [
        [lay.move(pieces[kn * lay.nd + kd], kd=kd, kn=kn) if kd or kn else pieces[0] for kd in range(lay.nd)]
        for kn in range(lay.near)
    ]
    cuts = wave_cut(lay, excitation, 0, (pieces[0],))
    inverse = over_near(lay, inverse_op)
    total = join(lay, got, (*cuts, part))
    past = from_behind(part, "delay", 1)
    direct = over_near(lay, operator)
    partial = invert(lay, along_col(lay, total), from_cores(lay, cuts), inverse)
    current, totals = apply(lay, over_rows(lay, partial), past, direct)
    cuts = wave_cut(lay, excitation, 1, (totals[-1],))
    total = join(lay, [[lay.move(block, kd=kd) if kd else block for kd, block in enumerate(totals)]], cuts)
    turned = turn(lay, over_near(lay, current))
    partial = invert(lay, along_col(lay, total), from_cores(lay, cuts), inverse, ())
    across = over_rows(lay, partial)
    last = join(lay, [across[kd :: lay.nd] for kd in range(lay.nd)])
    return tuple(finish(lay, [turned], over_near(lay, last)))


def on_device(excitation, delay_ops, inverse_op, history):
    sizes = [lax.axis_size(axis) for axis in ("delay", "row", "col")]
    steps, _, exc = excitation.shape
    follows = range(1, steps)
    share = exc // (sizes[0] * 2)
    if all(n & (n - 1) == 0 and n > 1 for n in sizes) and len(follows) == 1 and sizes[0] <= steps and share and share % TILE_ROWS == 0:
        return two_steps(excitation, delay_ops, inverse_op, history)
    return general(excitation, delay_ops, inverse_op, history)


def solution(mesh):
    in_specs = (
        P(None, "row", None),
        P("delay", "row", "col"),
        P("col", "row"),
        P("delay", "col", None),
    )
    out_specs = (P(None, "col", None), P("delay", "col", None))
    return jax.shard_map(
        on_device, mesh=mesh, in_specs=in_specs, out_specs=out_specs, check_vma=False
    )
```

```python
import functools

import jax
import jax.numpy as jnp
from jax import lax
from jax.experimental import pallas as pl
from jax.experimental.pallas import tpu as pltpu
from jax.sharding import PartitionSpec as P

F32 = jnp.float32
BF16 = jnp.bfloat16
TILE_ROWS = 16


def routes(axis):
    n = lax.axis_size(axis)
    if n & (n - 1) == 0:
        return [[(i, i ^ k) for i in range(n)] for k in range(1, n)]
    return [[(i, (i + k) % n) for i in range(n)] for k in range(1, n)]


def tree_sum(blocks):
    while len(blocks) > 1:
        pairs = [a + b for a, b in zip(blocks[::2], blocks[1::2])]
        blocks = pairs + ([blocks[-1]] if len(blocks) % 2 else [])
    return blocks[0]


def exchange_sum(block, axis):
    block = lax.optimization_barrier(block)
    blocks = [block] + [lax.ppermute(block, axis, route) for route in routes(axis)]
    return tree_sum([b.astype(F32) for b in blocks])


def piece(block, index, rows):
    return lax.dynamic_slice_in_dim(block, index * rows, rows, 0)


def scatter_sum(block, axis):
    n = lax.axis_size(axis)
    rows = block.shape[0] // n
    me = lax.axis_index(axis)
    parts = [piece(block, me, rows)]
    for route in routes(axis):
        target = jnp.array([t for _, t in route])[me]
        parts.append(lax.ppermute(piece(block, target, rows), axis, route))
    return tree_sum([p.astype(F32) for p in parts])


def gather(block, axis):
    n = lax.axis_size(axis)
    rows = block.shape[0]
    me = lax.axis_index(axis)
    whole = jnp.zeros((n * rows,) + block.shape[1:], block.dtype)
    whole = lax.dynamic_update_slice_in_dim(whole, block, me * rows, 0)
    for route in routes(axis):
        source = jnp.array([s for s, _ in sorted(route, key=lambda pair: pair[1])])[me]
        whole = lax.dynamic_update_slice_in_dim(whole, lax.ppermute(block, axis, route), source * rows, 0)
    return whole


def from_behind(block, axis, distance):
    n = lax.axis_size(axis)
    route = [(i - distance, i) for i in range(n) if i >= distance]
    return lax.ppermute(block, axis, route) if route else jnp.zeros_like(block)


def spread(block, axis, source):
    me = lax.axis_index(axis)
    out = block
    for target in range(lax.axis_size(axis)):
        if target != source:
            out = jnp.where(me == target, lax.ppermute(block, axis, [(source, target)]), out)
    return out


def times_transposed(a, b):
    return lax.dot_general(a, b, (((1,), (1,)), ((), ())), preferred_element_type=F32)


def general(excitation, delay_ops, inverse_op, history):
    steps, _, exc = excitation.shape
    operator, stored = delay_ops[0], history[0]
    nd = lax.axis_size("delay")
    me = lax.axis_index("delay")
    share = exc // nd
    stored_t = stored.T
    older = [scatter_sum(times_transposed(stored_t, operator).astype(BF16), "delay")]
    for step in range(1, steps):
        earlier = from_behind(stored_t, "delay", step)
        older.append(scatter_sum(times_transposed(earlier, operator).astype(BF16), "delay"))
    shortest = [spread(operator, "delay", lag) for lag in range(min(steps - 1, nd))]
    incident = [piece(excitation[step].T, me, share).astype(F32) for step in range(steps)]
    produced = []
    for step in range(steps):
        total = older[step]
        for lag in range(min(step, nd)):
            total = total + times_transposed(produced[step - 1 - lag], shortest[lag])
        retarded = exchange_sum(total.astype(BF16), "col")
        rhs = (incident[step] - retarded).astype(BF16)
        current = exchange_sum(times_transposed(rhs, inverse_op).astype(BF16), "row").astype(BF16)
        produced.append(current)
    whole = [gather(current, "delay").T for current in produced]
    currents = jnp.stack(whole)
    newest_first = jnp.stack(whole[::-1])
    picked = lax.dynamic_index_in_dim(newest_first, jnp.clip(me, 0, steps - 1), 0, keepdims=False)
    if nd > steps:
        picked = jnp.where(me < steps, picked, from_behind(stored, "delay", steps))
    return currents, picked[None]


class Layout:
    def __init__(self):
        self.nd = lax.axis_size("delay")
        self.nr = lax.axis_size("row")
        self.nc = lax.axis_size("col")
        self.near = 2 if self.nr % 2 == 0 else 1
        self.far = self.nr // self.near
        self.d = lax.axis_index("delay")
        self.n = lax.axis_index("row") % self.near
        self.z = lax.axis_index("col")

    def move(self, block, kd=0, kf=0, kn=0, kz=0, only=None):
        pairs = []
        for d in range(self.nd) if only is None else only:
            for r in range(self.nr):
                for z in range(self.nc):
                    to = ((d ^ kd) * self.nr + (r ^ (kf * self.near + kn))) * self.nc + (z ^ kz)
                    pairs.append(((d * self.nr + r) * self.nc + z, to))
        return lax.ppermute(block, ("delay", "row", "col"), pairs)


def farthest_first(body, numbers, loose, count, *refs):
    info, refs = [ref[0] for ref in refs[:numbers]], refs[numbers:]
    inputs = refs[loose : loose + count][::-1]
    body(loose, info, *refs[:loose], *inputs, *refs[loose + count :])


def kernel_call(body, out_shape, info, inputs, loose=(), scratch=()):
    vmem, smem = pl.BlockSpec(memory_space=pltpu.VMEM), pl.BlockSpec(memory_space=pltpu.SMEM)
    return pl.pallas_call(
        functools.partial(farthest_first, body, len(info), len(loose), len(inputs)),
        out_shape=out_shape,
        in_specs=[smem] * len(info) + [pl.BlockSpec(memory_space=pl.ANY)] * len(loose) + [vmem] * len(inputs),
        out_specs=jax.tree.map(lambda _: vmem, out_shape),
        scratch_shapes=list(scratch),
        cost_estimate=pl.CostEstimate(flops=1 << 28, bytes_accessed=1 << 20, transcendentals=0),
        compiler_params=pltpu.CompilerParams(vmem_limit_bytes=8 << 20),
    )(*[jnp.reshape(number, (1,)) for number in info], *loose, *inputs[::-1])


def owner(info, nd, k):
    return (info[1] ^ (k // nd)) * nd + (info[0] ^ (k % nd))


def total_of(refs):
    return tree_sum([ref[...].astype(F32) for ref in refs])


def part_of(ref, index, rows):
    return ref[pl.ds(pl.multiple_of(index * rows, rows), rows), :]


def begin_body(nd, loose, info, total_ref, *pieces):
    for k, piece in enumerate(pieces):
        piece[...] = part_of(total_ref, owner(info, nd, k), piece.shape[0])


def begin(lay, past, operator):
    total = lax.dot_general(past, operator, (((0,), (1,)), ((), ())), preferred_element_type=F32).astype(BF16)
    count = lay.near * lay.nd
    out = [jax.ShapeDtypeStruct((total.shape[0] // count, total.shape[1]), BF16)] * count
    return kernel_call(functools.partial(begin_body, lay.nd), out, [lay.d, lay.n], (total,))


def part_body(loose, info, *refs):
    past_ref, part_ref, turned = refs[loose:]
    turned[...] = past_ref[...].astype(F32).T
    part_ref[...] = part_of(turned, info[0], part_ref.shape[0]).astype(BF16)


def part_cut(lay, past, after):
    columns, exc = past.shape
    out = jax.ShapeDtypeStruct((exc // lay.near, columns), BF16)
    return kernel_call(part_body, out, [lay.n], (past,), after, [pltpu.VMEM((exc, columns), F32)])


def wave_body(step, nd, loose, info, *refs):
    incident_ref, outs, turned = refs[loose], refs[loose + 1 : -1], refs[-1]
    turned[...] = incident_ref[step].astype(F32).T
    for kn, out in enumerate(outs):
        out[...] = part_of(turned, owner(info, nd, kn * nd), out.shape[0]).astype(BF16)


def wave_cut(lay, incident, step, after):
    rows, exc = incident.shape[1:]
    out = [jax.ShapeDtypeStruct((exc // (lay.near * lay.nd), rows), BF16)] * lay.near
    body = functools.partial(wave_body, step, lay.nd)
    return kernel_call(body, out, [lay.d, lay.n], (incident,), after, [pltpu.VMEM((exc, rows), F32)])


def join_body(count, loose, info, *refs):
    ins, out = refs[loose:-1], refs[-1]
    rows = ins[0].shape[0]
    for k in range(count):
        out[pl.ds(k * rows, rows), :] = total_of(ins[k::count]).astype(BF16)


def join(lay, groups, loose=()):
    rows, columns = groups[0][0].shape
    out = jax.ShapeDtypeStruct((rows * len(groups), columns), BF16)
    flat = [block for blocks in zip(*groups) for block in blocks]
    return kernel_call(functools.partial(join_body, len(groups)), out, [lay.d], flat, loose)


def invert_body(near, loose, info, *refs):
    refs, out = refs[loose:-1], refs[-1]
    parts, waves, operators = refs[: -2 * near], refs[-2 * near : -near], refs[-near:]
    retarded = total_of(parts)
    rows = retarded.shape[0] // near
    terms = []
    for kn in range(near):
        rhs = (waves[kn][...].astype(F32) - retarded[kn * rows : (kn + 1) * rows]).astype(BF16)
        terms.append(times_transposed(rhs, operators[kn][...]))
    out[...] = tree_sum(terms).astype(BF16)


def invert(lay, parts, waves, operators, loose=()):
    out = jax.ShapeDtypeStruct((parts[0].shape[0] // lay.near, operators[0].shape[0]), BF16)
    body = functools.partial(invert_body, lay.near)
    return kernel_call(body, out, [lay.d], (*parts, *waves, *operators), loose)


def apply_body(near, nd, loose, info, *refs):
    refs = refs[loose:]
    refs, (current_ref, operand, *totals) = refs[: -1 - nd], refs[-1 - nd :]
    parts, past_ref, operators = refs[: -1 - near], refs[-1 - near], refs[-near:]
    rows = parts[0].shape[0]
    for kd in range(nd):
        current_ref[pl.ds(kd * rows, rows), :] = total_of(parts[kd::nd]).astype(BF16)

    @pl.when(info[0] == 0)
    def _():
        operand[...] = current_ref[...]

    @pl.when(info[0] != 0)
    def _():
        operand[...] = past_ref[...]

    for kd, total in enumerate(totals, 1):
        wanted = part_of(operand, info[0] ^ kd, rows)
        for kn in range(near):
            total[pl.ds(kn * rows, rows), :] = times_transposed(wanted, operators[kn][...]).astype(BF16)


def own_body(near, loose, info, *refs):
    operand, operators, total = refs[loose], refs[loose + 1 : -1], refs[-1]
    rows = total.shape[0] // near
    wanted = part_of(operand, info[0], rows)
    for kn in range(near):
        total[pl.ds(kn * rows, rows), :] = times_transposed(wanted, operators[kn][...]).astype(BF16)


def apply(lay, parts, past, operators):
    rows, columns = parts[0].shape
    total = jax.ShapeDtypeStruct((rows * lay.near, operators[0].shape[0]), BF16)
    out = [jax.ShapeDtypeStruct((rows * lay.nd, columns), BF16)] * 2 + [total] * (lay.nd - 1)
    body = functools.partial(apply_body, lay.near, lay.nd)
    current, operand, *others = kernel_call(body, out, [lay.d], (*parts, past, *operators))
    own = kernel_call(functools.partial(own_body, lay.near), total, [lay.d], (operand, *operators))
    return current, [own, *others]


def place(info, nd, blocks, total):
    rows = blocks[0].shape[0] // nd
    for k in range(total.shape[0] // rows):
        start = pl.multiple_of(owner(info, nd, k) * rows, rows)
        total[pl.ds(start, rows), :] = blocks[k // nd][pl.ds((k % nd) * rows, rows), :].astype(F32)
    return total[...].T.astype(BF16)


def turn_body(nd, loose, info, *refs):
    refs[-2][...] = place(info, nd, refs[loose:-2], refs[-1])


def turn(lay, blocks):
    columns, exc = blocks[0].shape[1], blocks[0].shape[0] * lay.near
    out = jax.ShapeDtypeStruct((columns, exc), BF16)
    scratch = [pltpu.VMEM((exc, columns), F32)]
    return kernel_call(functools.partial(turn_body, lay.nd), out, [lay.d, lay.n], blocks, (), scratch)


def finish_body(done, nd, d_ref, n_ref, *refs):
    info = [d_ref[0], n_ref[0]]
    earlier, blocks, (out, hist, total, turned, sems) = refs[:done], refs[done:-5], refs[-5:]

    def store(step, source):
        kept = pltpu.make_async_copy(source, hist.at[0], sems.at[done + 1])

        @pl.when(info[0] == done - step)
        def _():
            kept.start()

        copy = pltpu.make_async_copy(source, out.at[step], sems.at[step])
        copy.start()
        return copy, kept

    copies = [store(step, source) for step, source in enumerate(earlier)]
    turned[...] = place(info, nd, blocks, total)
    copies.append(store(done, turned))
    for copy, _ in copies:
        copy.wait()
    copies[-1][1].wait()


def finish(lay, earlier, blocks):
    done = len(earlier)
    columns, exc = earlier[0].shape
    hbm, vmem, smem = [pl.BlockSpec(memory_space=space) for space in (pltpu.HBM, pltpu.VMEM, pltpu.SMEM)]
    scratch = [pltpu.VMEM((exc, columns), F32), pltpu.VMEM((columns, exc), BF16), pltpu.SemaphoreType.DMA((done + 2,))]
    return pl.pallas_call(
        functools.partial(finish_body, done, lay.nd),
        out_shape=[jax.ShapeDtypeStruct((k, columns, exc), BF16) for k in (done + 1, 1)],
        in_specs=[smem] * 2 + [vmem] * (done + len(blocks)),
        out_specs=[hbm] * 2,
        scratch_shapes=scratch,
        compiler_params=pltpu.CompilerParams(vmem_limit_bytes=8 << 20),
    )(jnp.reshape(lay.d, (1,)), jnp.reshape(lay.n, (1,)), *earlier, *blocks)


def over_rows(lay, partial):
    return [
        lay.move(partial, kd=kd, kf=kf) if kd or kf else partial for kf in range(lay.far) for kd in range(lay.nd)
    ]


def over_near(lay, block):
    return [block] + [lay.move(block, kn=kn) for kn in range(1, lay.near)]


def along_col(lay, total):
    got = {kz: lay.move(total, kz=kz) for kz in reversed(range(1, lay.nc))}
    return [total] + [got[kz] for kz in range(1, lay.nc)]


def from_cores(lay, pieces):
    return [lay.move(piece, kn=kn) if kn else piece for kn, piece in enumerate(pieces)]


def two_steps(excitation, delay_ops, inverse_op, history):
    lay = Layout()
    operator, stored = delay_ops[0], history[0]
    pieces = begin(lay, stored, operator)
    part = part_cut(lay, stored, (pieces[0],))
    got = [
        [lay.move(pieces[kn * lay.nd + kd], kd=kd, kn=kn) if kd or kn else pieces[0] for kd in range(lay.nd)]
        for kn in range(lay.near)
    ]
    cuts = wave_cut(lay, excitation, 0, (pieces[0],))
    inverse = over_near(lay, inverse_op)
    total = join(lay, got, (*cuts, part))
    past = from_behind(part, "delay", 1)
    direct = over_near(lay, operator)
    partial = invert(lay, along_col(lay, total), from_cores(lay, cuts), inverse)
    current, totals = apply(lay, over_rows(lay, partial), past, direct)
    cuts = wave_cut(lay, excitation, 1, (totals[-1],))
    total = join(lay, [[lay.move(block, kd=kd) if kd else block for kd, block in enumerate(totals)]], cuts)
    turned = turn(lay, over_near(lay, current))
    partial = invert(lay, along_col(lay, total), from_cores(lay, cuts), inverse, ())
    across = over_rows(lay, partial)
    last = join(lay, [across[kd :: lay.nd] for kd in range(lay.nd)])
    return tuple(finish(lay, [turned], over_near(lay, last)))


def on_device(excitation, delay_ops, inverse_op, history):
    sizes = [lax.axis_size(axis) for axis in ("delay", "row", "col")]
    steps, _, exc = excitation.shape
    follows = range(1, steps)
    share = exc // (sizes[0] * 2)
    if all(n & (n - 1) == 0 and n > 1 for n in sizes) and len(follows) == 1 and sizes[0] <= steps and share and share % TILE_ROWS == 0:
        return two_steps(excitation, delay_ops, inverse_op, history)
    return general(excitation, delay_ops, inverse_op, history)


def solution(mesh):
    in_specs = (
        P(None, "row", None),
        P("delay", "row", "col"),
        P("col", "row"),
        P("delay", "col", None),
    )
    out_specs = (P(None, "col", None), P("delay", "col", None))
    return jax.shard_map(
        on_device, mesh=mesh, in_specs=in_specs, out_specs=out_specs, check_vma=False
    )
```
